128 devices in a mesh: occ: 4 (over z), virt: 32 (over y, x, core).
Axes of the slice: x: 4, y: 4, z: 4, core: 2. Of those that a mesh axis runs over, the one named last changes fastest.
Arguments:
- amplitudes: bfloat16 [256, 512, 512], P('occ', 'virt'), may hold values from -0.15625 to 0.15625
- ac_factor: bfloat16 [8, 512, 3072], P(None, ('virt', 'occ')), may hold values from -2 to 2
- bd_factor: bfloat16 [512, 128, 3072], P(('virt', 'occ')), may hold values from -2 to 2
- irrep_a: int32 [8], replicated, may hold values from 0 to 7
- irrep_b: int32 [128], replicated, may hold values from 0 to 7
- irrep_c: int32 [512], replicated, may hold values from 0 to 7
- irrep_d: int32 [512], P(('virt', 'occ')), may hold values from 0 to 7
Outputs:
- ladder: bfloat16 [256, 8, 128], P(('occ', 'virt'))
The draws below stay inside these ranges and needn't reach their ends.
All inputs are finite; a program needn't handle non-finite values.
Results may differ from the reference program's by a relative error of at most 0.0049.
Values may be sent and summed in bfloat16 or wider, within the bound.
No kernel may reach another device: no remote copies, remote signals or barrier semaphores. Data moves between devices by JAX's collectives and lax.ppermute only.
A program may use at most 128 MiB of HBM per device.

```python
import math
import jax
import jax.numpy as jnp
import numpy as np
from jax import lax

NQ = 3072
NA = 8
NB = 128
P_SIZE = 256
ND = 512
NC = 512
N_VIRT = 32


def place_ends(array, stream_key, smallest, largest):
    index_at = [jax.random.randint(jax.random.fold_in(stream_key, axis), (), 0, length) for axis, length in enumerate(array.shape)]
    widest = array.shape.index(max(array.shape))
    neighbour = index_at[:widest] + [(index_at[widest] + 1) % array.shape[widest]] + index_at[widest + 1:]
    return array.at[tuple(index_at)].set(smallest).at[tuple(neighbour)].set(largest)


def level_of(key, dims, cuts, smallest, largest):
    def one(dim, parts):
        steps = jax.random.uniform(jax.random.fold_in(jax.random.fold_in(key, 6), dim), (parts,), jnp.float32, smallest / len(cuts), largest / len(cuts))
        return jnp.repeat(jnp.exp(steps), dims[dim] // parts).reshape((-1,) + (1,) * (len(dims) - dim - 1))

    loudness = one(*cuts[0])
    for cut in cuts[1:]:
        loudness = loudness * one(*cut)
    return loudness


def rank_table(amount, slope):
    weights = [(1 << 20) // math.isqrt(grade ** slope) + 1 for grade in range(1, amount + 1)]
    spread = 1 + sum(weights) // (1 << 30)
    return np.cumsum(np.array([max(1, weight // spread) for weight in weights]))


def ranked_ids(key, extent, count, lean):
    table = rank_table(count, lean)
    ticket = jax.random.randint(jax.random.fold_in(key, 1), extent, 0, int(table[count - 1]))
    grade = jnp.searchsorted(jnp.asarray(table, jnp.int32), ticket, side="right")
    return jax.random.permutation(jax.random.fold_in(key, 2), count)[grade].astype(jnp.int32)


def normal_values(rng, extent, spread, reach, cuts=(), kind=jnp.bfloat16):
    result = jax.random.normal(rng, extent, jnp.float32) * spread
    if len(cuts) > 0:
        result = level_of(rng, extent, cuts, -0.22, 0.18) * result
    return jnp.clip(result, min=-reach, max=reach).astype(kind)


def setup_inputs(seed: int = 0) -> dict:
    key_of = jax.random.split(jax.random.key(seed), 8)
    amplitudes = normal_values(key_of[0], (P_SIZE, ND, NC), (2.0 * (8.0 / (NC * ND)) ** 0.5), 0.15625, ((0, 4), (1, 32)))
    ac_factor = normal_values(key_of[1], (NA, NC, NQ), (NQ ** -0.25), 2.0, ((1, 128),))
    bd_factor = normal_values(key_of[2], (ND, NB, NQ), (NQ ** -0.25), 2.0, ((0, 128),))
    irrep_a = place_ends(jax.random.randint(key_of[3], (NA,), 0, 8), jax.random.fold_in(key_of[3], 1), 0, 7).astype(jnp.int32)
    irrep_b = place_ends(jax.random.randint(key_of[4], (NB,), 0, 8), jax.random.fold_in(key_of[4], 1), 0, 7).astype(jnp.int32)
    irrep_c = place_ends(jax.random.randint(key_of[5], (NC,), 0, 8), jax.random.fold_in(key_of[5], 1), 0, 7).astype(jnp.int32)
    irrep_d = place_ends(ranked_ids(key_of[6], (ND,), 8, 2), jax.random.fold_in(key_of[6], 3), 0, 7).astype(jnp.int32)
    return dict(amplitudes=amplitudes, ac_factor=ac_factor, bd_factor=bd_factor, irrep_a=irrep_a, irrep_b=irrep_b, irrep_c=irrep_c, irrep_d=irrep_d)


def reference(amplitudes, ac_factor, bd_factor, irrep_a, irrep_b, irrep_c, irrep_d):
    width = ND // N_VIRT
    pair_ac = jnp.bitwise_xor(irrep_a[:, None], irrep_c[None, :])
    pair_bd = jnp.bitwise_xor(irrep_d[:, None], irrep_b[None, :])
    left = ac_factor.astype(jnp.float32)

    def step(total, index):
        start = (index * width).astype(jnp.int32)
        right = lax.dynamic_slice_in_dim(bd_factor, start, width, 0).astype(jnp.float32)
        amps = lax.dynamic_slice_in_dim(amplitudes, start, width, 1).astype(jnp.float32)
        labels = lax.dynamic_slice_in_dim(pair_bd, start, width, 0)
        integral = jnp.einsum('acq,dbq->acdb', left, right)
        keep = pair_ac[:, :, None, None] == labels[None, None, :, :]
        integral = jnp.where(keep, integral, jnp.float32(0.0)).astype(jnp.bfloat16)
        total = total + jnp.einsum('pdc,acdb->pab', amps, integral.astype(jnp.float32))
        return total, None

    start_total = jnp.zeros((P_SIZE, NA, NB), jnp.float32)
    total, unused = lax.scan(step, start_total, jnp.arange(N_VIRT, dtype=jnp.int32))
    return total.astype(jnp.bfloat16)
```

```python
import jax
import jax.numpy as jnp
from jax import lax
from jax.sharding import PartitionSpec as P


def body(amplitudes, ac_factor, bd_factor, irrep_a, irrep_b, irrep_c, irrep_d):
    left = lax.all_gather(ac_factor, ("virt", "occ"), axis=1, tiled=True)
    regrouped = lax.all_to_all(amplitudes, "occ", split_axis=1, concat_axis=0, tiled=True)
    pair_bd = jnp.bitwise_xor(irrep_d[:, None], irrep_b[None, :])
    pair_ac = jnp.bitwise_xor(irrep_a[:, None], irrep_c[None, :])
    integral = lax.dot_general(
        left, bd_factor, (((2,), (2,)), ((), ())), preferred_element_type=jnp.float32
    )
    keep = pair_ac[:, :, None, None] == pair_bd[None, None, :, :]
    integral = jnp.where(keep, integral, jnp.float32(0.0)).astype(jnp.bfloat16)
    total = jnp.einsum("pdc,acdb->pab", regrouped, integral, preferred_element_type=jnp.float32)
    pieces = total.astype(jnp.bfloat16).reshape(128, 2, total.shape[1], total.shape[2])
    pieces = lax.all_to_all(pieces, ("occ", "virt"), split_axis=0, concat_axis=0, tiled=True)
    return jnp.sum(pieces.astype(jnp.float32), axis=0).astype(jnp.bfloat16)


def solution(mesh):
    return jax.shard_map(
        body,
        mesh=mesh,
        in_specs=(
            P("occ", "virt", None),
            P(None, ("virt", "occ"), None),
            P(("virt", "occ"), None, None),
            P(),
            P(),
            P(),
            P(("virt", "occ")),
        ),
        out_specs=P(("occ", "virt"), None, None),
        check_vma=False,
    )
```

```python
import functools

import jax
import jax.numpy as jnp
from jax import lax
from jax.experimental import pallas as pl
from jax.experimental.pallas import tpu as pltpu
from jax.sharding import Mesh, PartitionSpec as P

ALL = ("zh", "zl", "y", "x", "core")
Z = ("zh", "zl")


def swap(block):
    return lax.ppermute(block, "core", [(0, 1), (1, 0)])


def around(block):
    pairs = [
        (z * 2 + core, (z + (1 - 2 * core)) % 4 * 2 + core) for z in range(4) for core in range(2)
    ]
    return lax.ppermute(block, Z + ("core",), pairs)


def along(block, axes):
    def moved(step):
        pairs = []
        for y in range(4):
            for x in range(4):
                for core in range(2):
                    to = ((y + step) % 4, x) if axes[core] == "y" else (y, (x + step) % 4)
                    pairs.append(((y * 4 + x) * 2 + core, (to[0] * 4 + to[1]) * 2 + core))
        return lax.ppermute(block, ("y", "x", "core"), pairs)

    return [moved(step) for step in (1, 3, 2)]


def part_kernel(amps, where, out, whole):
    spot = lax.broadcasted_iota(jnp.int32, (512, 512), 0)
    lane = lax.broadcasted_iota(jnp.int32, (512, 512), 1)
    z = lane // 8 % 2 * 2 + lane // 256
    place = lane // 64 % 4 * 128 + lane // 16 % 4 * 32 + lane // 4 % 2 * 16 + z * 4 + lane % 4
    pick = (spot == place).astype(jnp.bfloat16)
    for k in range(4):
        whole[k * 16 : k * 16 + 16] = jnp.dot(
            amps[k * 16 : k * 16 + 16].reshape(256, 512), pick, preferred_element_type=jnp.float32
        ).reshape(16, 16, 512)
    for z in range(4):
        lanes = slice(z % 2 * 256, z % 2 * 256 + 256)
        for j in range(4):
            out[z, j] = whole[:, 4 * z + j, lanes].astype(jnp.bfloat16)
        for core in range(2):

            @pl.when(where[3] == core)
            def _():
                near = (z + 2 * core - 1) % 4
                for j in range(4):
                    out[z, 4 + j] = whole[:, 4 * near + j, lanes].astype(jnp.bfloat16)


def part_amplitudes(amps, where):
    return pl.pallas_call(
        part_kernel,
        out_shape=jax.ShapeDtypeStruct((4, 8, 64, 256), jnp.bfloat16),
        in_specs=[pl.BlockSpec(memory_space=pltpu.VMEM), pl.BlockSpec(memory_space=pltpu.SMEM)],
        out_specs=pl.BlockSpec(memory_space=pltpu.VMEM),
        scratch_shapes=[pltpu.VMEM((64, 16, 512), jnp.float32)],
        compiler_params=pltpu.CompilerParams(vmem_limit_bytes=24 * 1024 * 1024),
        cost_estimate=pl.CostEstimate(flops=1 << 29, bytes_accessed=2 << 20, transcendentals=0),
    )(amps, where)


def corner(where, step, shift):
    y, x, core = where[0], where[1], where[3]
    far, near = (0, 3, 1, 2)[step], (0, 3, 1, 2)[shift] if isinstance(shift, int) else shift
    return (
        (y + jnp.where(core == 0, far, near)) % 4,
        (x + jnp.where(core == 0, near, far)) % 4,
    )


def fold_kernel(steps, offsets, *refs):
    n, n_groups = len(steps), len(offsets)
    blocks, refs = refs[:n], refs[n:]
    bds, amps, irreps = refs[:n_groups], refs[n_groups : 2 * n_groups], refs[2 * n_groups : 3 * n_groups]
    where, irrep_a, irrep_b, irrep_c, start, total, left, held, labels, sem = refs[3 * n_groups :]
    i = pl.program_id(0)

    @pl.when(i == 0)
    def _():
        copies = [
            pltpu.make_async_copy(block, left.at[pl.ds(256 * k, 256)], sem.at[k])
            for k, block in enumerate(blocks)
        ]
        for copy in copies:
            copy.start()
        total[...] = start[...]
        held[...] = jnp.zeros_like(held)
        row = lax.broadcasted_iota(jnp.int32, (256, 1), 0)
        shift, inner = row // 64, row % 16
        shift = jnp.where(shift == 1, 3, jnp.where(shift == 0, 0, shift - 1))
        lane = lax.broadcasted_iota(jnp.int32, (256, 512), 1)
        label_a = jnp.zeros((256, 1), jnp.int32)
        for a in range(4):
            label_a = jnp.where(row // 16 % 4 == a, irrep_a[where[3] * 4 + a], label_a)
        for k, step in enumerate(steps):
            y, x = corner(where, step, shift)
            z = inner // 8 * 2 + where[2]
            place = y * 128 + x * 32 + inner // 4 % 2 * 16 + z * 4 + inner % 4
            found = jnp.sum(
                jnp.where(lane == place, irrep_c[...].astype(jnp.float32), 0.0), axis=1, keepdims=True
            )
            labels[k * 256 : k * 256 + 256] = found.astype(jnp.int32) ^ label_a
        for copy in copies:
            copy.wait()

    for g in range(n_groups):
        for half in range(2):

            @pl.when(i == 2 * g + half)
            def _():
                integral = lax.dot_general(
                    left[...], bds[g][...].reshape(256, 3072), (((1,), (1,)), ((), ())),
                    preferred_element_type=jnp.float32,
                )
                pair = jnp.concatenate(
                    [irrep_b[...] ^ irreps[g][offsets[g] + 2 * half + d] for d in range(2)], axis=1
                )
                kept = jnp.where(labels[...] == pair, integral, 0.0).astype(jnp.bfloat16)
                for k, step in enumerate(steps):
                    for shift in range(4):
                        y, x = corner(where, step, shift)
                        to = pl.ds(pl.multiple_of(y * 64 + x * 16, 16), 16)
                        for a in range(4):
                            row = k * 256 + shift * 64 + a * 16
                            for d in range(2):
                                held[d, to, a * 128 : a * 128 + 128] = kept[
                                    row : row + 16, d * 128 : d * 128 + 128
                                ]
                total[...] += sum(
                    jnp.dot(
                        amps[g][:, d].reshape(256, 256), held[d], preferred_element_type=jnp.float32
                    )
                    for d in range(2)
                )


def fold(steps, blocks, groups, where, irrep_a, irrep_b, irrep_c, start):
    n, n_groups = len(steps), len(groups)
    rows = 256 * n
    smem, any_spec = pl.BlockSpec(memory_space=pltpu.SMEM), pl.BlockSpec(memory_space=pl.ANY)

    def half_of(g, i):
        return (jnp.clip(i - 2 * g, 0, 1), 0, 0)

    def amps_of(g, first, i):
        return (0, jnp.clip(i - 2 * g, 0, 1) + first, 0, 0)

    return pl.pallas_call(
        functools.partial(fold_kernel, steps, tuple(g[4] for g in groups)),
        grid=(2 * n_groups,),
        out_shape=jax.ShapeDtypeStruct((256, 512), jnp.float32),
        in_specs=[any_spec] * n
        + [pl.BlockSpec((2, 128, 3072), functools.partial(half_of, g)) for g in range(n_groups)]
        + [
            pl.BlockSpec((4, 2, 64, 256), functools.partial(amps_of, g, group[2]))
            for g, group in enumerate(groups)
        ]
        + [smem] * (n_groups + 2)
        + [
            pl.BlockSpec((1, 128), lambda i: (0, 0)),
            pl.BlockSpec((1, 512), lambda i: (0, 0)),
            pl.BlockSpec((256, 512), lambda i: (0, 0)),
        ],
        out_specs=pl.BlockSpec((256, 512), lambda i: (0, 0)),
        scratch_shapes=[
            pltpu.VMEM((rows, 3072), jnp.bfloat16),
            pltpu.VMEM((2, 256, 512), jnp.bfloat16),
            pltpu.VMEM((rows, 1), jnp.int32),
            pltpu.SemaphoreType.DMA((n,)),
        ],
        compiler_params=pltpu.CompilerParams(vmem_limit_bytes=30 * 1024 * 1024),
        cost_estimate=pl.CostEstimate(
            flops=2 * rows * 512 * n_groups * 3072, bytes_accessed=rows * 6144 + (n_groups * 3 << 20), transcendentals=0
        ),
    )(
        *[blocks[s] for s in steps], *[g[0] for g in groups], *[g[1] for g in groups],
        *[g[3] for g in groups], where, irrep_a, irrep_b, irrep_c, start,
    )


def body(amplitudes, ac_factor, bd_factor, irrep_a, irrep_b, irrep_c, irrep_d):
    where = jnp.stack([lax.axis_index(name) for name in ("y", "x", "zl", "core")]).astype(jnp.int32)
    zh, core = lax.axis_index("zh"), lax.axis_index("core")

    by_core = ac_factor.reshape(2, 16, 3072)
    mine = lax.dynamic_index_in_dim(by_core, core, 0, keepdims=False)
    theirs = lax.dynamic_index_in_dim(by_core, 1 - core, 0, keepdims=False)
    mine, theirs, amplitudes = lax.optimization_barrier((mine, theirs, amplitudes))
    from_core = swap(theirs)
    from_z = lax.ppermute(mine, "zh", [(0, 1), (1, 0)])
    from_both = lax.ppermute(theirs, ("zh", "core"), [(0, 3), (1, 2), (2, 1), (3, 0)])

    amps = part_amplitudes(amplitudes, where)
    near = around(irrep_d)
    other_far = swap(jnp.concatenate([irrep_d, near]))
    bd_core = swap(bd_factor)
    mine, from_core, from_z, from_both, amps, other_far, bd_sent = lax.optimization_barrier(
        (mine, from_core, from_z, from_both, amps, other_far, bd_factor)
    )

    amps = lax.all_to_all(amps, Z, split_axis=0, concat_axis=0, tiled=True)
    amps_other = swap(amps)

    first, second = jnp.where(core == 0, mine, from_core), jnp.where(core == 0, from_core, mine)
    third, fourth = jnp.where(core == 0, from_z, from_both), jnp.where(core == 0, from_both, from_z)
    pieces = jnp.stack([
        jnp.where(zh == 0, first, third), jnp.where(zh == 0, second, fourth),
        jnp.where(zh == 0, third, first), jnp.where(zh == 0, fourth, second),
    ])
    rows = pieces.reshape(4, 4, 4, 3072).transpose(1, 0, 2, 3).reshape(64, 3072)
    rows = jnp.concatenate([rows] + along(rows, "xy"), axis=0)
    blocks = [rows] + along(rows, "yx")

    bd_near = around(bd_sent)

    early = [(bd_factor, amps, 0, irrep_d, 0), (bd_core, amps_other, 0, other_far, 0)]
    rest = (where, irrep_a, irrep_b.reshape(1, 128), irrep_c.reshape(1, 512))
    total = jnp.zeros((256, 512), jnp.float32)
    total = fold((0, 1, 2), blocks, early, *rest, total)
    bd_near, total = lax.optimization_barrier((bd_near, total))
    bd_far = swap(bd_near)
    late = [(bd_near, amps, 2, near, 0), (bd_far, amps_other, 2, other_far, 4)]
    total = fold((0, 1, 2), blocks, late, *rest, total)
    total = fold((3,), blocks, early + late, *rest, total)

    pieces = total.astype(jnp.bfloat16).reshape(128, 2, 512)
    pieces = lax.all_to_all(pieces, ALL, split_axis=0, concat_axis=0, tiled=True)
    summed = jnp.sum(pieces.reshape(64, 2, 2, 512).astype(jnp.float32), axis=0)
    return summed.reshape(2, 2, 4, 128).transpose(1, 0, 2, 3).reshape(2, 8, 128).astype(jnp.bfloat16)


def solution(mesh):
    fine = Mesh(mesh.devices.reshape(2, 2, 4, 4, 2), ALL)
    virt = ("y", "x", "core")
    return jax.shard_map(
        body,
        mesh=fine,
        in_specs=(
            P(Z, virt, None),
            P(None, virt + Z, None),
            P(virt + Z, None, None),
            P(),
            P(),
            P(),
            P(virt + Z),
        ),
        out_specs=P(ALL, None, None),
        check_vma=False,
    )
```

```python
import functools

import jax
import jax.numpy as jnp
from jax import lax
from jax.experimental import pallas as pl
from jax.experimental.pallas import tpu as pltpu
from jax.sharding import Mesh, PartitionSpec as P

ALL = ("zh", "zl", "y", "x", "core")
Z = ("zh", "zl")


def swap(block):
    return lax.ppermute(block, "core", [(0, 1), (1, 0)])


def around(block):
    pairs = [
        (z * 2 + core, (z + (1 - 2 * core)) % 4 * 2 + core) for z in range(4) for core in range(2)
    ]
    return lax.ppermute(block, Z + ("core",), pairs)


def along(block, axes, steps=(1, 3, 2)):
    def moved(step):
        pairs = []
        for y in range(4):
            for x in range(4):
                for core in range(2):
                    to = ((y + step) % 4, x) if axes[core] == "y" else (y, (x + step) % 4)
                    pairs.append(((y * 4 + x) * 2 + core, (to[0] * 4 + to[1]) * 2 + core))
        return lax.ppermute(block, ("y", "x", "core"), pairs)

    return [moved(step) for step in steps]


def part_kernel(amps, where, own, one, two, three, whole):
    spot = lax.broadcasted_iota(jnp.int32, (512, 512), 0)
    lane = lax.broadcasted_iota(jnp.int32, (512, 512), 1)
    z = lane // 8 % 2 * 2 + lane // 256
    place = lane // 64 % 4 * 128 + lane // 16 % 4 * 32 + lane // 4 % 2 * 16 + z * 4 + lane % 4
    pick = (spot == place).astype(jnp.bfloat16)
    for k in range(4):
        picked = jnp.dot(
            amps[k * 16 : k * 16 + 16].reshape(256, 512), pick, preferred_element_type=jnp.float32
        )
        for role in range(2):
            whole[role, k * 16 : k * 16 + 16] = picked[:, role * 256 : role * 256 + 256].reshape(16, 16, 256)
    for step, out in enumerate((own, one, two, three)):
        z = (where[4] * 2 + where[2] + step) % 4
        near = (z + 2 * where[3] + 3) % 4
        for j in range(4):
            out[j] = whole[z % 2, :, 4 * z + j, :].astype(jnp.bfloat16)
            out[4 + j] = whole[z % 2, :, 4 * near + j, :].astype(jnp.bfloat16)


def part_amplitudes(amps, where):
    return pl.pallas_call(
        part_kernel,
        out_shape=[jax.ShapeDtypeStruct((8, 64, 256), jnp.bfloat16)] * 4,
        in_specs=[pl.BlockSpec(memory_space=pltpu.VMEM), pl.BlockSpec(memory_space=pltpu.SMEM)],
        out_specs=[pl.BlockSpec(memory_space=pltpu.VMEM)] * 4,
        scratch_shapes=[pltpu.VMEM((2, 64, 16, 256), jnp.float32)],
        compiler_params=pltpu.CompilerParams(vmem_limit_bytes=10 * 1024 * 1024),
        cost_estimate=pl.CostEstimate(flops=1 << 20, bytes_accessed=1 << 10, transcendentals=0),
    )(amps, where)


def order_kernel(own, one, two, three, where, out):
    for step, piece in enumerate((own, one, two, three)):
        out[(where[4] * 2 + where[2] + 4 - step) % 4] = piece[...]


def order_pairs(*args):
    smem, vmem = (pl.BlockSpec(memory_space=space) for space in (pltpu.SMEM, pltpu.VMEM))
    return pl.pallas_call(
        order_kernel,
        out_shape=jax.ShapeDtypeStruct((4, 8, 64, 256), jnp.bfloat16),
        in_specs=[vmem] * 4 + [smem],
        out_specs=vmem,
        compiler_params=pltpu.CompilerParams(vmem_limit_bytes=6 * 1024 * 1024),
        cost_estimate=pl.CostEstimate(flops=1 << 20, bytes_accessed=1 << 10, transcendentals=0),
    )(*args)


def halve_kernel(one, three, one_half, three_half):
    one_half[...] = one[:128]
    three_half[...] = three[128:]


def halve(*args):
    vmem = pl.BlockSpec(memory_space=pltpu.VMEM)
    return pl.pallas_call(
        halve_kernel,
        out_shape=[jax.ShapeDtypeStruct((128, 3072), jnp.bfloat16)] * 2,
        in_specs=[vmem] * 2,
        out_specs=[vmem] * 2,
        compiler_params=pltpu.CompilerParams(vmem_limit_bytes=6 * 1024 * 1024),
        cost_estimate=pl.CostEstimate(flops=1 << 20, bytes_accessed=1 << 10, transcendentals=0),
    )(*args)


def gather_kernel(mine, from_core, from_z, from_both, where, out):
    core, zh = where[3], where[4]
    same = [jnp.where(core == k, mine[...], from_core[...]) for k in range(2)]
    across = [jnp.where(core == k, from_z[...], from_both[...]) for k in range(2)]
    parts = [jnp.where(zh == k, same[c], across[c]) for k in range(2) for c in range(2)]
    for a in range(4):
        out[a * 16 : a * 16 + 16] = jnp.concatenate([part[a * 4 : a * 4 + 4] for part in parts], axis=0)


def gather_rows(*args):
    smem, vmem = (pl.BlockSpec(memory_space=space) for space in (pltpu.SMEM, pltpu.VMEM))
    return pl.pallas_call(
        gather_kernel,
        out_shape=jax.ShapeDtypeStruct((64, 3072), jnp.bfloat16),
        in_specs=[vmem] * 4 + [smem],
        out_specs=vmem,
        compiler_params=pltpu.CompilerParams(vmem_limit_bytes=6 * 1024 * 1024),
        cost_estimate=pl.CostEstimate(flops=1 << 20, bytes_accessed=1 << 10, transcendentals=0),
    )(*args)


def join_kernel(*refs):
    for k in range(4):
        refs[4][k * 64 : k * 64 + 64] = refs[k][...]


def join(pieces):
    vmem = pl.BlockSpec(memory_space=pltpu.VMEM)
    return pl.pallas_call(
        join_kernel,
        out_shape=jax.ShapeDtypeStruct((256, 3072), jnp.bfloat16),
        in_specs=[vmem] * 4,
        out_specs=vmem,
        compiler_params=pltpu.CompilerParams(vmem_limit_bytes=6 * 1024 * 1024),
        cost_estimate=pl.CostEstimate(flops=1 << 20, bytes_accessed=1 << 10, transcendentals=0),
    )(*pieces)


def corner(where, step, shift):
    y, x, core = where[0], where[1], where[3]
    far, near = (0, 3, 1, 2)[step], (0, 3, 1, 2)[shift] if isinstance(shift, int) else shift
    return (
        (y + jnp.where(core == 0, far, near)) % 4,
        (x + jnp.where(core == 0, near, far)) % 4,
    )


def integral_kernel(steps, chunks, counts, *refs):
    groups = []
    for count in counts:
        groups.append(refs[:count])
        refs = refs[count:]
    blocks, bds, irreps = groups
    where, irrep_a, irrep_b, irrep_c, held, labels, fourth = refs
    if 3 in steps:
        fourth[:128], fourth[128:] = blocks[-2][...], blocks[-1][...]
        blocks = [*blocks[:-2], fourth]

    if any(len(chunk[4]) < 4 for chunk in chunks):
        held[...] = jnp.zeros_like(held)
    row = lax.broadcasted_iota(jnp.int32, (256, 1), 0)
    shift, inner = row // 64, row % 16
    shift = jnp.where(shift == 1, 3, jnp.where(shift == 0, 0, shift - 1))
    lane = lax.broadcasted_iota(jnp.int32, (256, 512), 1)
    label_a = jnp.zeros((256, 1), jnp.int32)
    for a in range(4):
        label_a = jnp.where(row // 16 % 4 == a, irrep_a[where[3] * 4 + a], label_a)
    for k, step in enumerate(steps):
        y, x = corner(where, step, shift)
        z = inner // 8 * 2 + where[2]
        place = y * 128 + x * 32 + inner // 4 % 2 * 16 + z * 4 + inner % 4
        found = jnp.sum(
            jnp.where(lane == place, irrep_c[...].astype(jnp.float32), 0.0), axis=1, keepdims=True
        )
        labels[k * 256 : k * 256 + 256] = found.astype(jnp.int32) ^ label_a

    for i, (bd, bd_at, irrep, irrep_at, used) in enumerate(chunks):
        right = bds[bd][bd_at : bd_at + 2].reshape(256, 3072)
        pair = jnp.concatenate([irrep_b[...] ^ irreps[irrep][irrep_at + d] for d in range(2)], axis=1)
        for step in used:
            k = steps.index(step)
            integral = lax.dot_general(
                blocks[k][...], right, (((1,), (1,)), ((), ())), preferred_element_type=jnp.float32
            )
            same = labels[k * 256 : k * 256 + 256] == pair
            kept = jnp.where(same, integral, 0.0).astype(jnp.bfloat16)
            for shift in range(4):
                y, x = corner(where, step, shift)
                to = pl.ds(pl.multiple_of(y * 64 + x * 16, 16), 16)
                for a in range(4):
                    for d in range(2):
                        held[2 * i + d, to, a * 128 : a * 128 + 128] = kept[
                            shift * 64 + a * 16 : shift * 64 + a * 16 + 16, d * 128 : d * 128 + 128
                        ]


def integrals(blocks, pairs, where, irrep_a, irrep_b, irrep_c):
    arrays = [[], []]
    chunks = []
    for *pair, used in pairs:
        chunk = []
        for kind, (array, at) in zip(arrays, pair):
            if not any(array is known for known in kind):
                kind.append(array)
            chunk += [[array is known for known in kind].index(True), at]
        chunks.append((*chunk, used))
    steps = sorted({step for chunk in chunks for step in chunk[4]})
    pieces = [piece for s in steps for piece in blocks[s]]
    counts = (len(pieces), *[len(kind) for kind in arrays])
    smem, vmem = (pl.BlockSpec(memory_space=space) for space in (pltpu.SMEM, pltpu.VMEM))
    return pl.pallas_call(
        functools.partial(integral_kernel, tuple(steps), tuple(chunks), counts),
        out_shape=jax.ShapeDtypeStruct((2 * len(pairs), 256, 512), jnp.bfloat16),
        in_specs=[vmem] * sum(counts[:2]) + [smem] * (counts[2] + 2) + [vmem] * 2,
        out_specs=vmem,
        scratch_shapes=[
            pltpu.VMEM((256 * len(steps), 1), jnp.int32),
            pltpu.VMEM((256 if 3 in steps else 16, 3072), jnp.bfloat16),
        ],
        compiler_params=pltpu.CompilerParams(vmem_limit_bytes=12 * 1024 * 1024),
        cost_estimate=pl.CostEstimate(flops=1 << 20, bytes_accessed=1 << 10, transcendentals=0),
    )(*pieces, *arrays[0], *arrays[1], where, irrep_a, irrep_b, irrep_c)


def ladder_kernel(amps, amps_other, one, two, out):
    order = [(amps, d) for d in range(4)] + [(amps_other, d) for d in range(4)]
    order += [(t, 4 + d) for d0 in (0, 2) for t in (amps, amps_other) for d in (d0, d0 + 1)]
    left = jnp.concatenate([t[:, d].reshape(256, 256) for t, d in order], axis=1)
    n = one.shape[0] * 256
    total = jnp.dot(left[:, :n], one[...].reshape(n, 512), preferred_element_type=jnp.float32)
    total += jnp.dot(left, two[...].reshape(4096, 512), preferred_element_type=jnp.float32)
    out[...] = total.astype(out.dtype)


def ladder(*args):
    vmem = pl.BlockSpec(memory_space=pltpu.VMEM)
    return pl.pallas_call(
        ladder_kernel,
        out_shape=jax.ShapeDtypeStruct((256, 512), jnp.bfloat16),
        in_specs=[vmem] * 4,
        out_specs=vmem,
        compiler_params=pltpu.CompilerParams(vmem_limit_bytes=12 * 1024 * 1024),
        cost_estimate=pl.CostEstimate(flops=1 << 20, bytes_accessed=1 << 10, transcendentals=0),
    )(*args)


def body(amplitudes, ac_factor, bd_factor, irrep_a, irrep_b, irrep_c, irrep_d):
    where = jnp.stack([lax.axis_index(name) for name in ("y", "x", "zl", "core", "zh")]).astype(jnp.int32)
    core = lax.axis_index("core")

    by_core = ac_factor.reshape(2, 16, 3072)
    mine = lax.dynamic_index_in_dim(by_core, core, 0, keepdims=False)
    theirs = lax.dynamic_index_in_dim(by_core, 1 - core, 0, keepdims=False)
    from_core = swap(theirs)
    from_z = lax.ppermute(mine, "zh", [(0, 1), (1, 0)])
    from_both = lax.ppermute(theirs, ("zh", "core"), [(0, 3), (1, 2), (2, 1), (3, 0)])

    near = around(irrep_d)
    bd_core = swap(bd_factor)
    mine, from_core, from_z, from_both, near_irreps, bd_core, bd_first, bd_last = lax.optimization_barrier(
        (mine, from_core, from_z, from_both, jnp.concatenate([irrep_d, near]), bd_core, bd_factor[:2], bd_factor[2:])
    )

    rows = gather_rows(mine, from_core, from_z, from_both, where)
    lines = along(rows, "xy")
    near_first, near_last = around(bd_first), around(bd_last)
    other_far = swap(near_irreps)
    rows = join([rows] + lines)
    rows, amplitudes = lax.optimization_barrier((rows, amplitudes))
    one, three = along(rows, "yx", (1, 3))

    parted = part_amplitudes(amplitudes, where)
    one, three, near_first, *parted = lax.optimization_barrier((one, three, near_first, *parted))
    parted = [
        lax.ppermute(part, Z, [(z, (z + step) % 4) for z in range(4)]) if step else part
        for step, part in enumerate(parted)
    ]

    far_first = swap(near_first)
    one_half, three_half = halve(one, three)
    (two_first,) = along(one_half, "yx", (1,))
    (two_last,) = along(three_half, "yx", (3,))

    rest = (where, irrep_a, irrep_b.reshape(1, 128), irrep_c.reshape(1, 512))
    blocks = [[rows], [one], [three], [two_first, two_last]]
    first = [((bd_factor, at), (near_irreps, at)) for at in (0, 2)]
    first += [((bd_core, at), (other_far, at)) for at in (0, 2)]
    first += [((near_first, 0), (near_irreps, 4))]
    held_first = integrals(blocks, [(*pair, (0, 1, 2)) for pair in first], *rest)
    near_last, held_first, two_first, two_last, far_first = lax.optimization_barrier(
        (near_last, held_first, two_first, two_last, far_first)
    )
    blocks[3] = [two_first, two_last]
    far_last = swap(near_last)
    last = [((far_first, 0), (other_far, 4)), ((near_last, 0), (near_irreps, 6)), ((far_last, 0), (other_far, 6))]
    held_last = integrals(
        blocks, [(*pair, (3,)) for pair in first] + [(*pair, (0, 1, 2, 3)) for pair in last], *rest
    )
    held_last, *parted = lax.optimization_barrier((held_last, *parted))
    amps = order_pairs(*parted, where)
    amps_other = swap(amps)
    total = ladder(amps, amps_other, held_first, held_last)

    pieces = total.reshape(128, 2, 512)
    pieces = lax.all_to_all(pieces, ALL, split_axis=0, concat_axis=0, tiled=True)
    summed = jnp.sum(pieces.reshape(64, 2, 2, 512).astype(jnp.float32), axis=0)
    return summed.reshape(2, 2, 4, 128).transpose(1, 0, 2, 3).reshape(2, 8, 128).astype(jnp.bfloat16)


def solution(mesh):
    fine = Mesh(mesh.devices.reshape(2, 2, 4, 4, 2), ALL)
    virt = ("y", "x", "core")
    return jax.shard_map(
        body,
        mesh=fine,
        in_specs=(
            P(Z, virt, None),
            P(None, virt + Z, None),
            P(virt + Z, None, None),
            P(),
            P(),
            P(),
            P(virt + Z),
        ),
        out_specs=P(ALL, None, None),
        check_vma=False,
    )
```

```python
import functools

import jax
import jax.numpy as jnp
from jax import lax
from jax.experimental import pallas as pl
from jax.experimental.pallas import tpu as pltpu
from jax.sharding import Mesh, PartitionSpec as P

ALL = ("zh", "zl", "y", "x", "core")
Z = ("zh", "zl")


def swap(block):
    return lax.ppermute(block, "core", [(0, 1), (1, 0)])


def around(block):
    pairs = [
        (z * 2 + core, (z + (1 - 2 * core)) % 4 * 2 + core) for z in range(4) for core in range(2)
    ]
    return lax.ppermute(block, Z + ("core",), pairs)


def along(block, axes, steps=(1, 3, 2)):
    def moved(step):
        pairs = []
        for y in range(4):
            for x in range(4):
                for core in range(2):
                    to = ((y + step) % 4, x) if axes[core] == "y" else (y, (x + step) % 4)
                    pairs.append(((y * 4 + x) * 2 + core, (to[0] * 4 + to[1]) * 2 + core))
        return lax.ppermute(block, ("y", "x", "core"), pairs)

    return [moved(step) for step in steps]


def part_kernel(amps, where, own, one, two, three, whole):
    spot = lax.broadcasted_iota(jnp.int32, (512, 512), 0)
    lane = lax.broadcasted_iota(jnp.int32, (512, 512), 1)
    z = lane // 8 % 2 * 2 + lane // 256
    place = lane // 64 % 4 * 128 + lane // 16 % 4 * 32 + lane // 4 % 2 * 16 + z * 4 + lane % 4
    pick = (spot == place).astype(jnp.bfloat16)
    for k in range(4):
        picked = jnp.dot(
            amps[k * 16 : k * 16 + 16].reshape(256, 512), pick, preferred_element_type=jnp.float32
        )
        for role in range(2):
            whole[role, k * 16 : k * 16 + 16] = picked[:, role * 256 : role * 256 + 256].reshape(16, 16, 256)
    for step, out in enumerate((own, one, two, three)):
        z = (where[4] * 2 + where[2] + step) % 4
        near = (z + 2 * where[3] + 3) % 4
        for j in range(4):
            out[j] = whole[z % 2, :, 4 * z + j, :].astype(jnp.bfloat16)
            out[4 + j] = whole[z % 2, :, 4 * near + j, :].astype(jnp.bfloat16)


def part_amplitudes(amps, where):
    return pl.pallas_call(
        part_kernel,
        out_shape=[jax.ShapeDtypeStruct((8, 64, 256), jnp.bfloat16)] * 4,
        in_specs=[pl.BlockSpec(memory_space=pltpu.VMEM), pl.BlockSpec(memory_space=pltpu.SMEM)],
        out_specs=[pl.BlockSpec(memory_space=pltpu.VMEM)] * 4,
        scratch_shapes=[pltpu.VMEM((2, 64, 16, 256), jnp.float32)],
        compiler_params=pltpu.CompilerParams(vmem_limit_bytes=10 * 1024 * 1024),
        cost_estimate=pl.CostEstimate(flops=1 << 20, bytes_accessed=1 << 10, transcendentals=0),
    )(amps, where)


def order_kernel(own, one, two, three, where, out):
    for step, piece in enumerate((own, one, two, three)):
        out[(where[4] * 2 + where[2] + 4 - step) % 4] = piece[...]


def order_pairs(*args):
    smem, vmem = (pl.BlockSpec(memory_space=space) for space in (pltpu.SMEM, pltpu.VMEM))
    return pl.pallas_call(
        order_kernel,
        out_shape=jax.ShapeDtypeStruct((4, 8, 64, 256), jnp.bfloat16),
        in_specs=[vmem] * 4 + [smem],
        out_specs=vmem,
        compiler_params=pltpu.CompilerParams(vmem_limit_bytes=6 * 1024 * 1024),
        cost_estimate=pl.CostEstimate(flops=1 << 20, bytes_accessed=1 << 10, transcendentals=0),
    )(*args)


def halve_kernel(one, three, one_half, three_half):
    one_half[...] = one[:128]
    three_half[...] = three[128:]


def halve(*args):
    vmem = pl.BlockSpec(memory_space=pltpu.VMEM)
    return pl.pallas_call(
        halve_kernel,
        out_shape=[jax.ShapeDtypeStruct((128, 3072), jnp.bfloat16)] * 2,
        in_specs=[vmem] * 2,
        out_specs=[vmem] * 2,
        compiler_params=pltpu.CompilerParams(vmem_limit_bytes=6 * 1024 * 1024),
        cost_estimate=pl.CostEstimate(flops=1 << 20, bytes_accessed=1 << 10, transcendentals=0),
    )(*args)


def gather_kernel(mine, from_core, from_z, from_both, where, out):
    core, zh = where[3], where[4]
    same = [jnp.where(core == k, mine[...], from_core[...]) for k in range(2)]
    across = [jnp.where(core == k, from_z[...], from_both[...]) for k in range(2)]
    parts = [jnp.where(zh == k, same[c], across[c]) for k in range(2) for c in range(2)]
    for a in range(4):
        out[a * 16 : a * 16 + 16] = jnp.concatenate([part[a * 4 : a * 4 + 4] for part in parts], axis=0)


def gather_rows(*args):
    smem, vmem = (pl.BlockSpec(memory_space=space) for space in (pltpu.SMEM, pltpu.VMEM))
    return pl.pallas_call(
        gather_kernel,
        out_shape=jax.ShapeDtypeStruct((64, 3072), jnp.bfloat16),
        in_specs=[vmem] * 4 + [smem],
        out_specs=vmem,
        compiler_params=pltpu.CompilerParams(vmem_limit_bytes=6 * 1024 * 1024),
        cost_estimate=pl.CostEstimate(flops=1 << 20, bytes_accessed=1 << 10, transcendentals=0),
    )(*args)


def join_kernel(*refs):
    for k in range(4):
        refs[4][k * 64 : k * 64 + 64] = refs[k][...]


def join(pieces):
    vmem = pl.BlockSpec(memory_space=pltpu.VMEM)
    return pl.pallas_call(
        join_kernel,
        out_shape=jax.ShapeDtypeStruct((256, 3072), jnp.bfloat16),
        in_specs=[vmem] * 4,
        out_specs=vmem,
        compiler_params=pltpu.CompilerParams(vmem_limit_bytes=6 * 1024 * 1024),
        cost_estimate=pl.CostEstimate(flops=1 << 20, bytes_accessed=1 << 10, transcendentals=0),
    )(*pieces)


def corner(where, step, shift):
    y, x, core = where[0], where[1], where[3]
    far, near = (0, 3, 1, 2)[step], (0, 3, 1, 2)[shift] if isinstance(shift, int) else shift
    return (
        (y + jnp.where(core == 0, far, near)) % 4,
        (x + jnp.where(core == 0, near, far)) % 4,
    )


def integral_kernel(steps, chunks, counts, *refs):
    groups = []
    for count in counts:
        groups.append(refs[:count])
        refs = refs[count:]
    blocks, bds, irreps = groups
    where, irrep_a, irrep_b, irrep_c, *base, held, labels, fourth = refs
    if 3 in steps:
        fourth[:128], fourth[128:] = blocks[-2][...], blocks[-1][...]
        blocks = [*blocks[:-2], fourth]

    done = base[0].shape[0] if base else 0
    if base:
        held[:done] = base[0][...]
    if done < held.shape[0]:
        held[done:] = jnp.zeros((held.shape[0] - done, 256, 512), jnp.bfloat16)
    row = lax.broadcasted_iota(jnp.int32, (256, 1), 0)
    shift, inner = row // 64, row % 16
    shift = jnp.where(shift == 1, 3, jnp.where(shift == 0, 0, shift - 1))
    lane = lax.broadcasted_iota(jnp.int32, (256, 512), 1)
    label_a = jnp.zeros((256, 1), jnp.int32)
    for a in range(4):
        label_a = jnp.where(row // 16 % 4 == a, irrep_a[where[3] * 4 + a], label_a)
    for k, step in enumerate(steps):
        y, x = corner(where, step, shift)
        z = inner // 8 * 2 + where[2]
        place = y * 128 + x * 32 + inner // 4 % 2 * 16 + z * 4 + inner % 4
        found = jnp.sum(
            jnp.where(lane == place, irrep_c[...].astype(jnp.float32), 0.0), axis=1, keepdims=True
        )
        labels[k * 256 : k * 256 + 256] = found.astype(jnp.int32) ^ label_a

    for i, (bd, bd_at, irrep, irrep_at, used) in enumerate(chunks):
        right = bds[bd][bd_at : bd_at + 2].reshape(256, 3072)
        pair = jnp.concatenate([irrep_b[...] ^ irreps[irrep][irrep_at + d] for d in range(2)], axis=1)
        for step in used:
            k = steps.index(step)
            integral = lax.dot_general(
                blocks[k][...], right, (((1,), (1,)), ((), ())), preferred_element_type=jnp.float32
            )
            same = labels[k * 256 : k * 256 + 256] == pair
            kept = jnp.where(same, integral, 0.0).astype(jnp.bfloat16)
            for shift in range(4):
                y, x = corner(where, step, shift)
                to = pl.ds(pl.multiple_of(y * 64 + x * 16, 16), 16)
                for a in range(4):
                    for d in range(2):
                        held[2 * i + d, to, a * 128 : a * 128 + 128] = kept[
                            shift * 64 + a * 16 : shift * 64 + a * 16 + 16, d * 128 : d * 128 + 128
                        ]


def integrals(blocks, pairs, where, irrep_a, irrep_b, irrep_c, base=()):
    arrays = [[], []]
    chunks = []
    for *pair, used in pairs:
        chunk = []
        for kind, (array, at) in zip(arrays, pair):
            if not any(array is known for known in kind):
                kind.append(array)
            chunk += [[array is known for known in kind].index(True), at]
        chunks.append((*chunk, used))
    steps = sorted({step for chunk in chunks for step in chunk[4]})
    pieces = [piece for s in steps for piece in blocks[s]]
    counts = (len(pieces), *[len(kind) for kind in arrays])
    smem, vmem = (pl.BlockSpec(memory_space=space) for space in (pltpu.SMEM, pltpu.VMEM))
    return pl.pallas_call(
        functools.partial(integral_kernel, tuple(steps), tuple(chunks), counts),
        out_shape=jax.ShapeDtypeStruct((2 * len(pairs), 256, 512), jnp.bfloat16),
        in_specs=[vmem] * sum(counts[:2]) + [smem] * (counts[2] + 2) + [vmem] * (2 + len(base)),
        out_specs=vmem,
        scratch_shapes=[
            pltpu.VMEM((256 * len(steps), 1), jnp.int32),
            pltpu.VMEM((256 if 3 in steps else 16, 3072), jnp.bfloat16),
        ],
        compiler_params=pltpu.CompilerParams(vmem_limit_bytes=12 * 1024 * 1024),
        cost_estimate=pl.CostEstimate(flops=1 << 20, bytes_accessed=1 << 10, transcendentals=0),
    )(*pieces, *arrays[0], *arrays[1], where, irrep_a, irrep_b, irrep_c, *base)


def ladder_kernel(amps, amps_other, held, out):
    order = [(amps, d) for d in range(4)] + [(amps_other, d) for d in range(4)]
    order += [(t, 4 + d) for d0 in (0, 2) for t in (amps, amps_other) for d in (d0, d0 + 1)]
    left = jnp.concatenate([t[:, d].reshape(256, 256) for t, d in order], axis=1)
    total = jnp.dot(left, held[...].reshape(4096, 512), preferred_element_type=jnp.float32)
    out[...] = total.astype(out.dtype)


def ladder(*args):
    vmem = pl.BlockSpec(memory_space=pltpu.VMEM)
    return pl.pallas_call(
        ladder_kernel,
        out_shape=jax.ShapeDtypeStruct((256, 512), jnp.bfloat16),
        in_specs=[vmem] * 3,
        out_specs=vmem,
        compiler_params=pltpu.CompilerParams(vmem_limit_bytes=12 * 1024 * 1024),
        cost_estimate=pl.CostEstimate(flops=1 << 20, bytes_accessed=1 << 10, transcendentals=0),
    )(*args)


def body(amplitudes, ac_factor, bd_factor, irrep_a, irrep_b, irrep_c, irrep_d):
    where = jnp.stack([lax.axis_index(name) for name in ("y", "x", "zl", "core", "zh")]).astype(jnp.int32)
    core = lax.axis_index("core")

    by_core = ac_factor.reshape(2, 16, 3072)
    mine = lax.dynamic_index_in_dim(by_core, core, 0, keepdims=False)
    theirs = lax.dynamic_index_in_dim(by_core, 1 - core, 0, keepdims=False)
    from_core = swap(theirs)
    from_z = lax.ppermute(mine, "zh", [(0, 1), (1, 0)])
    from_both = lax.ppermute(theirs, ("zh", "core"), [(0, 3), (1, 2), (2, 1), (3, 0)])

    near = around(irrep_d)
    bd_core = swap(bd_factor)
    mine, from_core, from_z, from_both, near_irreps, bd_core, bd_first, bd_last = lax.optimization_barrier(
        (mine, from_core, from_z, from_both, jnp.concatenate([irrep_d, near]), bd_core, bd_factor[:2], bd_factor[2:])
    )

    rows = gather_rows(mine, from_core, from_z, from_both, where)
    lines = along(rows, "xy")
    near_first, near_last = around(bd_first), around(bd_last)
    other_far = swap(near_irreps)
    rows = join([rows] + lines)
    rows, amplitudes, other_far = lax.optimization_barrier((rows, amplitudes, other_far))
    one, three = along(rows, "yx", (1, 3))

    parted = part_amplitudes(amplitudes, where)
    rest = (where, irrep_a, irrep_b.reshape(1, 128), irrep_c.reshape(1, 512))
    first = [((bd_factor, at), (near_irreps, at)) for at in (0, 2)]
    first += [((bd_core, at), (other_far, at)) for at in (0, 2)]
    held = integrals([[rows]], [(*pair, (0,)) for pair in first], *rest)
    far_first = swap(near_first)
    one, three, far_first, near_last, held, *parted = lax.optimization_barrier(
        (one, three, far_first, near_last, held, *parted)
    )
    parted = [
        lax.ppermute(part, Z, [(z, (z + step) % 4) for z in range(4)]) if step else part
        for step, part in enumerate(parted)
    ]

    one_half, three_half = halve(one, three)
    (two_first,) = along(one_half, "yx", (1,))
    (two_last,) = along(three_half, "yx", (3,))

    blocks = [[rows], [one], [three], [two_first, two_last]]
    close = [((near_first, 0), (near_irreps, 4)), ((far_first, 0), (other_far, 4))]
    far_last = swap(near_last)
    close += [((near_last, 0), (near_irreps, 6)), ((far_last, 0), (other_far, 6))]
    held = integrals(
        blocks, [(*pair, (1, 2)) for pair in first] + [(*pair, (0, 1, 2)) for pair in close], *rest, (held,)
    )
    held, two_first, two_last, parted[2] = lax.optimization_barrier((held, two_first, two_last, parted[2]))
    blocks[3] = [two_first, two_last]
    held = integrals(blocks, [(*pair, (3,)) for pair in first + close], *rest, (held,))
    held, *parted = lax.optimization_barrier((held, *parted))
    amps = order_pairs(*parted, where)
    amps_other = swap(amps)
    total = ladder(amps, amps_other, held)

    pieces = total.reshape(128, 2, 512)
    pieces = lax.all_to_all(pieces, ALL, split_axis=0, concat_axis=0, tiled=True)
    summed = jnp.sum(pieces.reshape(64, 2, 2, 512).astype(jnp.float32), axis=0)
    return summed.reshape(2, 2, 4, 128).transpose(1, 0, 2, 3).reshape(2, 8, 128).astype(jnp.bfloat16)


def solution(mesh):
    fine = Mesh(mesh.devices.reshape(2, 2, 4, 4, 2), ALL)
    virt = ("y", "x", "core")
    return jax.shard_map(
        body,
        mesh=fine,
        in_specs=(
            P(Z, virt, None),
            P(None, virt + Z, None),
            P(virt + Z, None, None),
            P(),
            P(),
            P(),
            P(virt + Z),
        ),
        out_specs=P(ALL, None, None),
        check_vma=False,
    )
```

```python
import functools

import jax
import jax.numpy as jnp
from jax import lax
from jax.experimental import pallas as pl
from jax.experimental.pallas import tpu as pltpu
from jax.sharding import Mesh, PartitionSpec as P

ALL = ("zh", "zl", "y", "x", "core")
Z = ("zh", "zl")


def swap(block):
    return lax.ppermute(block, "core", [(0, 1), (1, 0)])


def around(block):
    pairs = [
        (z * 2 + core, (z + (1 - 2 * core)) % 4 * 2 + core) for z in range(4) for core in range(2)
    ]
    return lax.ppermute(block, Z + ("core",), pairs)


def along(block, axes, steps=(1, 3, 2)):
    def moved(step):
        pairs = []
        for y in range(4):
            for x in range(4):
                for core in range(2):
                    to = ((y + step) % 4, x) if axes[core] == "y" else (y, (x + step) % 4)
                    pairs.append(((y * 4 + x) * 2 + core, (to[0] * 4 + to[1]) * 2 + core))
        return lax.ppermute(block, ("y", "x", "core"), pairs)

    return [moved(step) for step in steps]


def part_kernel(amps, where, own, one, two, three, whole):
    spot = lax.broadcasted_iota(jnp.int32, (512, 512), 0)
    lane = lax.broadcasted_iota(jnp.int32, (512, 512), 1)
    z = lane // 8 % 2 * 2 + lane // 256
    place = lane // 64 % 4 * 128 + lane // 16 % 4 * 32 + lane // 4 % 2 * 16 + z * 4 + lane % 4
    pick = (spot == place).astype(jnp.bfloat16)
    for k in range(4):
        picked = jnp.dot(
            amps[k * 16 : k * 16 + 16].reshape(256, 512), pick, preferred_element_type=jnp.float32
        )
        for role in range(2):
            whole[role, k * 16 : k * 16 + 16] = picked[:, role * 256 : role * 256 + 256].reshape(16, 16, 256)
    for step, out in enumerate((own, one, two, three)):
        z = (where[4] * 2 + where[2] + step) % 4
        near = (z + 2 * where[3] + 3) % 4
        for j in range(4):
            out[j] = whole[z % 2, :, 4 * z + j, :].astype(jnp.bfloat16)
            out[4 + j] = whole[z % 2, :, 4 * near + j, :].astype(jnp.bfloat16)


def part_amplitudes(amps, where):
    return pl.pallas_call(
        part_kernel,
        out_shape=[jax.ShapeDtypeStruct((8, 64, 256), jnp.bfloat16)] * 4,
        in_specs=[pl.BlockSpec(memory_space=pltpu.VMEM), pl.BlockSpec(memory_space=pltpu.SMEM)],
        out_specs=[pl.BlockSpec(memory_space=pltpu.VMEM)] * 4,
        scratch_shapes=[pltpu.VMEM((2, 64, 16, 256), jnp.float32)],
        compiler_params=pltpu.CompilerParams(vmem_limit_bytes=10 * 1024 * 1024),
        cost_estimate=pl.CostEstimate(flops=1 << 20, bytes_accessed=1 << 10, transcendentals=0),
    )(amps, where)


def order_kernel(own, one, two, three, where, out):
    for step, piece in enumerate((own, one, two, three)):
        out[(where[4] * 2 + where[2] + 4 - step) % 4] = piece[...]


def order_pairs(*args):
    smem, vmem = (pl.BlockSpec(memory_space=space) for space in (pltpu.SMEM, pltpu.VMEM))
    return pl.pallas_call(
        order_kernel,
        out_shape=jax.ShapeDtypeStruct((4, 8, 64, 256), jnp.bfloat16),
        in_specs=[vmem] * 4 + [smem],
        out_specs=vmem,
        compiler_params=pltpu.CompilerParams(vmem_limit_bytes=6 * 1024 * 1024),
        cost_estimate=pl.CostEstimate(flops=1 << 20, bytes_accessed=1 << 10, transcendentals=0),
    )(*args)


def halve_kernel(one, three, one_half, three_half):
    one_half[...] = one[:128]
    three_half[...] = three[128:]


def halve(*args):
    vmem = pl.BlockSpec(memory_space=pltpu.VMEM)
    return pl.pallas_call(
        halve_kernel,
        out_shape=[jax.ShapeDtypeStruct((128, 3072), jnp.bfloat16)] * 2,
        in_specs=[vmem] * 2,
        out_specs=[vmem] * 2,
        compiler_params=pltpu.CompilerParams(vmem_limit_bytes=6 * 1024 * 1024),
        cost_estimate=pl.CostEstimate(flops=1 << 20, bytes_accessed=1 << 10, transcendentals=0),
    )(*args)


def gather_kernel(mine, from_core, from_z, from_both, where, out):
    core, zh = where[3], where[4]
    same = [jnp.where(core == k, mine[...], from_core[...]) for k in range(2)]
    across = [jnp.where(core == k, from_z[...], from_both[...]) for k in range(2)]
    parts = [jnp.where(zh == k, same[c], across[c]) for k in range(2) for c in range(2)]
    for a in range(4):
        out[a * 16 : a * 16 + 16] = jnp.concatenate([part[a * 4 : a * 4 + 4] for part in parts], axis=0)


def gather_rows(*args):
    smem, vmem = (pl.BlockSpec(memory_space=space) for space in (pltpu.SMEM, pltpu.VMEM))
    return pl.pallas_call(
        gather_kernel,
        out_shape=jax.ShapeDtypeStruct((64, 3072), jnp.bfloat16),
        in_specs=[vmem] * 4 + [smem],
        out_specs=vmem,
        compiler_params=pltpu.CompilerParams(vmem_limit_bytes=6 * 1024 * 1024),
        cost_estimate=pl.CostEstimate(flops=1 << 20, bytes_accessed=1 << 10, transcendentals=0),
    )(*args)


def join_kernel(*refs):
    for k in range(4):
        refs[4][k * 64 : k * 64 + 64] = refs[k][...]


def join(pieces):
    vmem = pl.BlockSpec(memory_space=pltpu.VMEM)
    return pl.pallas_call(
        join_kernel,
        out_shape=jax.ShapeDtypeStruct((256, 3072), jnp.bfloat16),
        in_specs=[vmem] * 4,
        out_specs=vmem,
        compiler_params=pltpu.CompilerParams(vmem_limit_bytes=6 * 1024 * 1024),
        cost_estimate=pl.CostEstimate(flops=1 << 20, bytes_accessed=1 << 10, transcendentals=0),
    )(*pieces)


def corner(where, step, shift):
    y, x, core = where[0], where[1], where[3]
    far, near = (0, 3, 1, 2)[step], (0, 3, 1, 2)[shift] if isinstance(shift, int) else shift
    return (
        (y + jnp.where(core == 0, far, near)) % 4,
        (x + jnp.where(core == 0, near, far)) % 4,
    )


def integral_kernel(steps, chunks, counts, *refs):
    groups = []
    for count in counts:
        groups.append(refs[:count])
        refs = refs[count:]
    blocks, bds, irreps = groups
    where, irrep_a, irrep_b, irrep_c, *base, held, labels, fourth = refs
    if 3 in steps:
        fourth[:128], fourth[128:] = blocks[-2][...], blocks[-1][...]
        blocks = [*blocks[:-2], fourth]

    done = base[0].shape[0] if base else 0
    if base:
        held[:done] = base[0][...]
    if done < held.shape[0]:
        held[done:] = jnp.zeros((held.shape[0] - done, 256, 512), jnp.bfloat16)
    row = lax.broadcasted_iota(jnp.int32, (256, 1), 0)
    shift, inner = row // 64, row % 16
    shift = jnp.where(shift == 1, 3, jnp.where(shift == 0, 0, shift - 1))
    lane = lax.broadcasted_iota(jnp.int32, (256, 512), 1)
    label_a = jnp.zeros((256, 1), jnp.int32)
    for a in range(4):
        label_a = jnp.where(row // 16 % 4 == a, irrep_a[where[3] * 4 + a], label_a)
    for k, step in enumerate(steps):
        y, x = corner(where, step, shift)
        z = inner // 8 * 2 + where[2]
        place = y * 128 + x * 32 + inner // 4 % 2 * 16 + z * 4 + inner % 4
        found = jnp.sum(
            jnp.where(lane == place, irrep_c[...].astype(jnp.float32), 0.0), axis=1, keepdims=True
        )
        labels[k * 256 : k * 256 + 256] = found.astype(jnp.int32) ^ label_a

    for i, (bd, bd_at, irrep, irrep_at, used) in enumerate(chunks):
        right = bds[bd][bd_at : bd_at + 2].reshape(256, 3072)
        pair = jnp.concatenate([irrep_b[...] ^ irreps[irrep][irrep_at + d] for d in range(2)], axis=1)
        for step in used:
            k = steps.index(step)
            integral = lax.dot_general(
                blocks[k][...], right, (((1,), (1,)), ((), ())), preferred_element_type=jnp.float32
            )
            same = labels[k * 256 : k * 256 + 256] == pair
            kept = jnp.where(same, integral, 0.0).astype(jnp.bfloat16)
            for shift in range(4):
                y, x = corner(where, step, shift)
                to = pl.ds(pl.multiple_of(y * 64 + x * 16, 16), 16)
                for a in range(4):
                    for d in range(2):
                        held[2 * i + d, to, a * 128 : a * 128 + 128] = kept[
                            shift * 64 + a * 16 : shift * 64 + a * 16 + 16, d * 128 : d * 128 + 128
                        ]


def integrals(blocks, pairs, where, irrep_a, irrep_b, irrep_c, base=()):
    arrays = [[], []]
    chunks = []
    for *pair, used in pairs:
        chunk = []
        for kind, (array, at) in zip(arrays, pair):
            if not any(array is known for known in kind):
                kind.append(array)
            chunk += [[array is known for known in kind].index(True), at]
        chunks.append((*chunk, used))
    steps = sorted({step for chunk in chunks for step in chunk[4]})
    pieces = [piece for s in steps for piece in blocks[s]]
    counts = (len(pieces), *[len(kind) for kind in arrays])
    smem, vmem = (pl.BlockSpec(memory_space=space) for space in (pltpu.SMEM, pltpu.VMEM))
    return pl.pallas_call(
        functools.partial(integral_kernel, tuple(steps), tuple(chunks), counts),
        out_shape=jax.ShapeDtypeStruct((2 * len(pairs), 256, 512), jnp.bfloat16),
        in_specs=[vmem] * sum(counts[:2]) + [smem] * (counts[2] + 2) + [vmem] * (2 + len(base)),
        out_specs=vmem,
        scratch_shapes=[
            pltpu.VMEM((256 * len(steps), 1), jnp.int32),
            pltpu.VMEM((256 if 3 in steps else 16, 3072), jnp.bfloat16),
        ],
        compiler_params=pltpu.CompilerParams(vmem_limit_bytes=12 * 1024 * 1024),
        cost_estimate=pl.CostEstimate(flops=1 << 20, bytes_accessed=1 << 10, transcendentals=0),
    )(*pieces, *arrays[0], *arrays[1], where, irrep_a, irrep_b, irrep_c, *base)


def ladder_kernel(amps, amps_other, held, out):
    order = [(amps, d) for d in range(4)] + [(amps_other, d) for d in range(4)]
    order += [(t, 4 + d) for d0 in (0, 2) for t in (amps, amps_other) for d in (d0, d0 + 1)]
    left = jnp.concatenate([t[:, d].reshape(256, 256) for t, d in order], axis=1)
    total = jnp.dot(left, held[...].reshape(4096, 512), preferred_element_type=jnp.float32)
    out[...] = total.astype(out.dtype)


def ladder(*args):
    vmem = pl.BlockSpec(memory_space=pltpu.VMEM)
    return pl.pallas_call(
        ladder_kernel,
        out_shape=jax.ShapeDtypeStruct((256, 512), jnp.bfloat16),
        in_specs=[vmem] * 3,
        out_specs=vmem,
        compiler_params=pltpu.CompilerParams(vmem_limit_bytes=12 * 1024 * 1024),
        cost_estimate=pl.CostEstimate(flops=1 << 20, bytes_accessed=1 << 10, transcendentals=0),
    )(*args)


def body(amplitudes, ac_factor, bd_factor, irrep_a, irrep_b, irrep_c, irrep_d):
    where = jnp.stack([lax.axis_index(name) for name in ("y", "x", "zl", "core", "zh")]).astype(jnp.int32)
    core = lax.axis_index("core")

    by_core = ac_factor.reshape(2, 16, 3072)
    mine = lax.dynamic_index_in_dim(by_core, core, 0, keepdims=False)
    theirs = lax.dynamic_index_in_dim(by_core, 1 - core, 0, keepdims=False)
    from_core = swap(theirs)
    from_z = lax.ppermute(mine, "zh", [(0, 1), (1, 0)])
    from_both = lax.ppermute(theirs, ("zh", "core"), [(0, 3), (1, 2), (2, 1), (3, 0)])

    near = around(irrep_d)
    bd_core = swap(bd_factor)
    mine, from_core, from_z, from_both, near_irreps, bd_core, bd_first, bd_last = lax.optimization_barrier(
        (mine, from_core, from_z, from_both, jnp.concatenate([irrep_d, near]), bd_core, bd_factor[:2], bd_factor[2:])
    )

    rows = gather_rows(mine, from_core, from_z, from_both, where)
    lines = along(rows, "xy")
    near_first, near_last = around(bd_first), around(bd_last)
    other_far = swap(near_irreps)
    rows = join([rows] + lines)
    rows, amplitudes, other_far = lax.optimization_barrier((rows, amplitudes, other_far))
    one, three = along(rows, "yx", (1, 3))

    parted = part_amplitudes(amplitudes, where)
    rest = (where, irrep_a, irrep_b.reshape(1, 128), irrep_c.reshape(1, 512))
    first = [((bd_factor, at), (near_irreps, at)) for at in (0, 2)]
    first += [((bd_core, at), (other_far, at)) for at in (0, 2)]
    held = integrals([[rows]], [(*pair, (0,)) for pair in first], *rest)
    far_first = swap(near_first)
    one, three, far_first, near_last, held, *parted = lax.optimization_barrier(
        (one, three, far_first, near_last, held, *parted)
    )
    parted = [
        lax.ppermute(part, Z, [(z, (z + step) % 4) for z in range(4)]) if step else part
        for step, part in enumerate(parted)
    ]

    one_half, three_half = halve(one, three)
    (two_first,) = along(one_half, "yx", (1,))
    (two_last,) = along(three_half, "yx", (3,))

    blocks = [[rows], [one], [three], [two_first, two_last]]
    close = [((near_first, 0), (near_irreps, 4)), ((far_first, 0), (other_far, 4))]
    far_last = swap(near_last)
    close += [((near_last, 0), (near_irreps, 6)), ((far_last, 0), (other_far, 6))]
    held = integrals(
        blocks, [(*pair, (1, 2)) for pair in first] + [(*pair, (0, 1, 2)) for pair in close], *rest, (held,)
    )
    held, two_first, two_last, *parted = lax.optimization_barrier((held, two_first, two_last, *parted))
    blocks[3] = [two_first, two_last]
    amps = order_pairs(*parted, where)
    held, amps = lax.optimization_barrier((held, amps))
    amps_other = swap(amps)
    held = integrals(blocks, [(*pair, (3,)) for pair in first + close], *rest, (held,))
    total = ladder(amps, amps_other, held)

    pieces = total.reshape(128, 2, 512)
    pieces = lax.all_to_all(pieces, ALL, split_axis=0, concat_axis=0, tiled=True)
    summed = jnp.sum(pieces.reshape(64, 2, 2, 512).astype(jnp.float32), axis=0)
    return summed.reshape(2, 2, 4, 128).transpose(1, 0, 2, 3).reshape(2, 8, 128).astype(jnp.bfloat16)


def solution(mesh):
    fine = Mesh(mesh.devices.reshape(2, 2, 4, 4, 2), ALL)
    virt = ("y", "x", "core")
    return jax.shard_map(
        body,
        mesh=fine,
        in_specs=(
            P(Z, virt, None),
            P(None, virt + Z, None),
            P(virt + Z, None, None),
            P(),
            P(),
            P(),
            P(virt + Z),
        ),
        out_specs=P(ALL, None, None),
        check_vma=False,
    )
```

```python
import functools

import jax
import jax.numpy as jnp
from jax import lax
from jax.experimental import pallas as pl
from jax.experimental.pallas import tpu as pltpu
from jax.sharding import Mesh, PartitionSpec as P

ALL = ("zh", "zl", "y", "x", "core")
Z = ("zh", "zl")


def swap(block):
    return lax.ppermute(block, "core", [(0, 1), (1, 0)])


def around(block):
    pairs = [
        (z * 2 + core, (z + (1 - 2 * core)) % 4 * 2 + core) for z in range(4) for core in range(2)
    ]
    return lax.ppermute(block, Z + ("core",), pairs)


def along(block, axes, steps=(1, 3, 2)):
    def moved(step):
        pairs = []
        for y in range(4):
            for x in range(4):
                for core in range(2):
                    to = ((y + step) % 4, x) if axes[core] == "y" else (y, (x + step) % 4)
                    pairs.append(((y * 4 + x) * 2 + core, (to[0] * 4 + to[1]) * 2 + core))
        return lax.ppermute(block, ("y", "x", "core"), pairs)

    return [moved(step) for step in steps]


def part_kernel(amps, where, own, one, two, three, whole):
    spot = lax.broadcasted_iota(jnp.int32, (512, 512), 0)
    lane = lax.broadcasted_iota(jnp.int32, (512, 512), 1)
    z = lane // 8 % 2 * 2 + lane // 256
    place = lane // 64 % 4 * 128 + lane // 16 % 4 * 32 + lane // 4 % 2 * 16 + z * 4 + lane % 4
    pick = (spot == place).astype(jnp.bfloat16)
    for k in range(4):
        picked = jnp.dot(
            amps[k * 16 : k * 16 + 16].reshape(256, 512), pick, preferred_element_type=jnp.float32
        )
        for role in range(2):
            whole[role, k * 16 : k * 16 + 16] = picked[:, role * 256 : role * 256 + 256].reshape(16, 16, 256)
    for step, out in enumerate((own, one, two, three)):
        z = (where[4] * 2 + where[2] + step) % 4
        near = (z + 2 * where[3] + 3) % 4
        for j in range(4):
            out[j] = whole[z % 2, :, 4 * z + j, :].astype(jnp.bfloat16)
            out[4 + j] = whole[z % 2, :, 4 * near + j, :].astype(jnp.bfloat16)


def part_amplitudes(amps, where):
    return pl.pallas_call(
        part_kernel,
        out_shape=[jax.ShapeDtypeStruct((8, 64, 256), jnp.bfloat16)] * 4,
        in_specs=[pl.BlockSpec(memory_space=pltpu.VMEM), pl.BlockSpec(memory_space=pltpu.SMEM)],
        out_specs=[pl.BlockSpec(memory_space=pltpu.VMEM)] * 4,
        scratch_shapes=[pltpu.VMEM((2, 64, 16, 256), jnp.float32)],
        compiler_params=pltpu.CompilerParams(vmem_limit_bytes=10 * 1024 * 1024),
        cost_estimate=pl.CostEstimate(flops=1 << 20, bytes_accessed=1 << 10, transcendentals=0),
    )(amps, where)


def order_kernel(own, one, two, three, where, out):
    for step, piece in enumerate((own, one, two, three)):
        out[(where[4] * 2 + where[2] + 4 - step) % 4] = piece[...]


def order_pairs(*args):
    smem, vmem = (pl.BlockSpec(memory_space=space) for space in (pltpu.SMEM, pltpu.VMEM))
    return pl.pallas_call(
        order_kernel,
        out_shape=jax.ShapeDtypeStruct((4, 8, 64, 256), jnp.bfloat16),
        in_specs=[vmem] * 4 + [smem],
        out_specs=vmem,
        compiler_params=pltpu.CompilerParams(vmem_limit_bytes=6 * 1024 * 1024),
        cost_estimate=pl.CostEstimate(flops=1 << 20, bytes_accessed=1 << 10, transcendentals=0),
    )(*args)


def halve_kernel(one, three, one_half, three_half):
    one_half[...] = one[:128]
    three_half[...] = three[128:]


def halve(*args):
    vmem = pl.BlockSpec(memory_space=pltpu.VMEM)
    return pl.pallas_call(
        halve_kernel,
        out_shape=[jax.ShapeDtypeStruct((128, 3072), jnp.bfloat16)] * 2,
        in_specs=[vmem] * 2,
        out_specs=[vmem] * 2,
        compiler_params=pltpu.CompilerParams(vmem_limit_bytes=6 * 1024 * 1024),
        cost_estimate=pl.CostEstimate(flops=1 << 20, bytes_accessed=1 << 10, transcendentals=0),
    )(*args)


def gather_kernel(mine, from_core, from_z, from_both, where, out):
    core, zh = where[3], where[4]
    same = [jnp.where(core == k, mine[...], from_core[...]) for k in range(2)]
    across = [jnp.where(core == k, from_z[...], from_both[...]) for k in range(2)]
    parts = [jnp.where(zh == k, same[c], across[c]) for k in range(2) for c in range(2)]
    for a in range(4):
        out[a * 16 : a * 16 + 16] = jnp.concatenate([part[a * 4 : a * 4 + 4] for part in parts], axis=0)


def gather_rows(*args):
    smem, vmem = (pl.BlockSpec(memory_space=space) for space in (pltpu.SMEM, pltpu.VMEM))
    return pl.pallas_call(
        gather_kernel,
        out_shape=jax.ShapeDtypeStruct((64, 3072), jnp.bfloat16),
        in_specs=[vmem] * 4 + [smem],
        out_specs=vmem,
        compiler_params=pltpu.CompilerParams(vmem_limit_bytes=6 * 1024 * 1024),
        cost_estimate=pl.CostEstimate(flops=1 << 20, bytes_accessed=1 << 10, transcendentals=0),
    )(*args)


def join_kernel(*refs):
    for k in range(4):
        refs[4][k * 64 : k * 64 + 64] = refs[k][...]


def join(pieces):
    vmem = pl.BlockSpec(memory_space=pltpu.VMEM)
    return pl.pallas_call(
        join_kernel,
        out_shape=jax.ShapeDtypeStruct((256, 3072), jnp.bfloat16),
        in_specs=[vmem] * 4,
        out_specs=vmem,
        compiler_params=pltpu.CompilerParams(vmem_limit_bytes=6 * 1024 * 1024),
        cost_estimate=pl.CostEstimate(flops=1 << 20, bytes_accessed=1 << 10, transcendentals=0),
    )(*pieces)


def corner(where, step, shift):
    y, x, core = where[0], where[1], where[3]
    far, near = (0, 3, 1, 2)[step], (0, 3, 1, 2)[shift] if isinstance(shift, int) else shift
    return (
        (y + jnp.where(core == 0, far, near)) % 4,
        (x + jnp.where(core == 0, near, far)) % 4,
    )


def integral_kernel(steps, chunks, counts, *refs):
    groups = []
    for count in counts:
        groups.append(refs[:count])
        refs = refs[count:]
    blocks, bds, irreps = groups
    where, irrep_a, irrep_b, irrep_c, *base, held, labels, fourth = refs
    if 3 in steps:
        fourth[:128], fourth[128:] = blocks[-2][...], blocks[-1][...]
        blocks = [*blocks[:-2], fourth]

    done = base[0].shape[0] if base else 0
    if base:
        held[:done] = base[0][...]
    if done < held.shape[0]:
        held[done:] = jnp.zeros((held.shape[0] - done, 256, 512), jnp.bfloat16)
    row = lax.broadcasted_iota(jnp.int32, (256, 1), 0)
    shift, inner = row // 64, row % 16
    shift = jnp.where(shift == 1, 3, jnp.where(shift == 0, 0, shift - 1))
    lane = lax.broadcasted_iota(jnp.int32, (256, 512), 1)
    label_a = jnp.zeros((256, 1), jnp.int32)
    for a in range(4):
        label_a = jnp.where(row // 16 % 4 == a, irrep_a[where[3] * 4 + a], label_a)
    for k, step in enumerate(steps):
        y, x = corner(where, step, shift)
        z = inner // 8 * 2 + where[2]
        place = y * 128 + x * 32 + inner // 4 % 2 * 16 + z * 4 + inner % 4
        found = jnp.sum(
            jnp.where(lane == place, irrep_c[...].astype(jnp.float32), 0.0), axis=1, keepdims=True
        )
        labels[k * 256 : k * 256 + 256] = found.astype(jnp.int32) ^ label_a

    for i, (bd, bd_at, irrep, irrep_at, used) in enumerate(chunks):
        right = bds[bd][bd_at : bd_at + 2].reshape(256, 3072)
        pair = jnp.concatenate([irrep_b[...] ^ irreps[irrep][irrep_at + d] for d in range(2)], axis=1)
        for step in used:
            k = steps.index(step)
            integral = lax.dot_general(
                blocks[k][...], right, (((1,), (1,)), ((), ())), preferred_element_type=jnp.float32
            )
            same = labels[k * 256 : k * 256 + 256] == pair
            kept = jnp.where(same, integral, 0.0).astype(jnp.bfloat16)
            for shift in range(4):
                y, x = corner(where, step, shift)
                to = pl.ds(pl.multiple_of(y * 64 + x * 16, 16), 16)
                for a in range(4):
                    for d in range(2):
                        held[2 * i + d, to, a * 128 : a * 128 + 128] = kept[
                            shift * 64 + a * 16 : shift * 64 + a * 16 + 16, d * 128 : d * 128 + 128
                        ]


def integrals(blocks, pairs, where, irrep_a, irrep_b, irrep_c, base=()):
    arrays = [[], []]
    chunks = []
    for *pair, used in pairs:
        chunk = []
        for kind, (array, at) in zip(arrays, pair):
            if not any(array is known for known in kind):
                kind.append(array)
            chunk += [[array is known for known in kind].index(True), at]
        chunks.append((*chunk, used))
    steps = sorted({step for chunk in chunks for step in chunk[4]})
    pieces = [piece for s in steps for piece in blocks[s]]
    counts = (len(pieces), *[len(kind) for kind in arrays])
    smem, vmem = (pl.BlockSpec(memory_space=space) for space in (pltpu.SMEM, pltpu.VMEM))
    return pl.pallas_call(
        functools.partial(integral_kernel, tuple(steps), tuple(chunks), counts),
        out_shape=jax.ShapeDtypeStruct((2 * len(pairs), 256, 512), jnp.bfloat16),
        in_specs=[vmem] * sum(counts[:2]) + [smem] * (counts[2] + 2) + [vmem] * (2 + len(base)),
        out_specs=vmem,
        scratch_shapes=[
            pltpu.VMEM((256 * len(steps), 1), jnp.int32),
            pltpu.VMEM((256 if 3 in steps else 16, 3072), jnp.bfloat16),
        ],
        compiler_params=pltpu.CompilerParams(vmem_limit_bytes=12 * 1024 * 1024),
        cost_estimate=pl.CostEstimate(flops=1 << 20, bytes_accessed=1 << 10, transcendentals=0),
    )(*pieces, *arrays[0], *arrays[1], where, irrep_a, irrep_b, irrep_c, *base)


def ladder_kernel(amps, amps_other, held, out):
    order = [(amps, d) for d in range(4)] + [(amps_other, d) for d in range(4)]
    order += [(t, 4 + d) for d0 in (0, 2) for t in (amps, amps_other) for d in (d0, d0 + 1)]
    left = jnp.concatenate([t[:, d].reshape(256, 256) for t, d in order], axis=1)
    total = jnp.dot(left, held[...].reshape(4096, 512), preferred_element_type=jnp.float32)
    out[...] = total.astype(out.dtype)


def ladder(*args):
    vmem = pl.BlockSpec(memory_space=pltpu.VMEM)
    return pl.pallas_call(
        ladder_kernel,
        out_shape=jax.ShapeDtypeStruct((256, 512), jnp.bfloat16),
        in_specs=[vmem] * 3,
        out_specs=vmem,
        compiler_params=pltpu.CompilerParams(vmem_limit_bytes=12 * 1024 * 1024),
        cost_estimate=pl.CostEstimate(flops=1 << 20, bytes_accessed=1 << 10, transcendentals=0),
    )(*args)


def body(amplitudes, ac_factor, bd_factor, irrep_a, irrep_b, irrep_c, irrep_d):
    where = jnp.stack([lax.axis_index(name) for name in ("y", "x", "zl", "core", "zh")]).astype(jnp.int32)
    core = lax.axis_index("core")

    by_core = ac_factor.reshape(2, 16, 3072)
    mine = lax.dynamic_index_in_dim(by_core, core, 0, keepdims=False)
    theirs = lax.dynamic_index_in_dim(by_core, 1 - core, 0, keepdims=False)
    from_core = swap(theirs)
    from_z = lax.ppermute(mine, "zh", [(0, 1), (1, 0)])
    from_both = lax.ppermute(theirs, ("zh", "core"), [(0, 3), (1, 2), (2, 1), (3, 0)])

    near = around(irrep_d)
    bd_core = swap(bd_factor)
    mine, from_core, from_z, from_both, near_irreps, bd_core, bd_first, bd_last = lax.optimization_barrier(
        (mine, from_core, from_z, from_both, jnp.concatenate([irrep_d, near]), bd_core, bd_factor[:2], bd_factor[2:])
    )

    rows = gather_rows(mine, from_core, from_z, from_both, where)
    lines = along(rows, "xy")
    near_first, near_last = around(bd_first), around(bd_last)
    other_far = swap(near_irreps)
    rows = join([rows] + lines)
    rows, amplitudes, other_far = lax.optimization_barrier((rows, amplitudes, other_far))
    one, three = along(rows, "yx", (1, 3))

    parted = part_amplitudes(amplitudes, where)
    rest = (where, irrep_a, irrep_b.reshape(1, 128), irrep_c.reshape(1, 512))
    first = [((bd_factor, at), (near_irreps, at)) for at in (0, 2)]
    first += [((bd_core, at), (other_far, at)) for at in (0, 2)]
    far_first = swap(near_first)
    first += [((near_first, 0), (near_irreps, 4))]
    held = integrals([[rows]], [(*pair, (0,)) for pair in first], *rest)
    one, three, far_first, near_last, held, *parted = lax.optimization_barrier(
        (one, three, far_first, near_last, held, *parted)
    )
    parted = [
        lax.ppermute(part, Z, [(z, (z + step) % 4) for z in range(4)]) if step else part
        for step, part in enumerate(parted)
    ]

    one_half, three_half = halve(one, three)
    (two_first,) = along(one_half, "yx", (1,))
    (two_last,) = along(three_half, "yx", (3,))

    blocks = [[rows], [one], [three], [two_first, two_last]]
    close = [((far_first, 0), (other_far, 4))]
    far_last = swap(near_last)
    close += [((near_last, 0), (near_irreps, 6)), ((far_last, 0), (other_far, 6))]
    held = integrals(
        blocks, [(*pair, (1, 2)) for pair in first] + [(*pair, (0, 1, 2)) for pair in close], *rest, (held,)
    )
    held, two_first, two_last, *parted = lax.optimization_barrier((held, two_first, two_last, *parted))
    blocks[3] = [two_first, two_last]
    amps = order_pairs(*parted, where)
    held, amps = lax.optimization_barrier((held, amps))
    amps_other = swap(amps)
    held = integrals(blocks, [(*pair, (3,)) for pair in first + close], *rest, (held,))
    total = ladder(amps, amps_other, held)

    pieces = total.reshape(128, 2, 512)
    pieces = lax.all_to_all(pieces, ALL, split_axis=0, concat_axis=0, tiled=True)
    summed = jnp.sum(pieces.reshape(64, 2, 2, 512).astype(jnp.float32), axis=0)
    return summed.reshape(2, 2, 4, 128).transpose(1, 0, 2, 3).reshape(2, 8, 128).astype(jnp.bfloat16)


def solution(mesh):
    fine = Mesh(mesh.devices.reshape(2, 2, 4, 4, 2), ALL)
    virt = ("y", "x", "core")
    return jax.shard_map(
        body,
        mesh=fine,
        in_specs=(
            P(Z, virt, None),
            P(None, virt + Z, None),
            P(virt + Z, None, None),
            P(),
            P(),
            P(),
            P(virt + Z),
        ),
        out_specs=P(ALL, None, None),
        check_vma=False,
    )
```
